256 devices in a mesh: seq: 32 (over y, z), mp: 8 (over x, core).
Axes of the slice: x: 4, y: 4, z: 8, core: 2. Of those that a mesh axis runs over, the one named last changes fastest.
Arguments:
- queries: bfloat16 [16384, 6144], P('seq', 'mp'), may hold values from -8 to 8
- keys: bfloat16 [16384, 6144], P('seq', 'mp'), may hold values from -8 to 8
- values: bfloat16 [16384, 6144], P('seq', 'mp'), may hold values from -10 to 10
- residual: bfloat16 [16384, 6144], P('seq', 'mp'), may hold values from -42 to 42
- out_weight: bfloat16 [6144, 6144], P('mp', 'seq'), may hold values from -0.078125 to 0.078125
- gate: bfloat16 [32, 6144], P(None, 'mp'), may hold values from -4 to 4
- mod_scale: bfloat16 [32, 6144], P(None, 'mp'), may hold values from -2.5 to 2.5
- mod_shift: bfloat16 [32, 6144], P(None, 'mp'), may hold values from -4 to 4
- frame_counts: int32 [32], replicated, may hold values from 1 to 8, 128 in all
- patch_counts: int32 [32], replicated, may hold values from 32 to 128, as said below
Outputs:
- updated: bfloat16 [16384, 6144], P('seq', 'mp')
- normed: bfloat16 [16384, 6144], P('seq', 'mp')
The draws below stay inside these ranges and needn't reach their ends.
Inputs may be any that keep to these rules, and one draw needn't show every extreme that they name: `patch_counts`: some clip has 128 live cells a frame.
All inputs are finite; a program needn't handle non-finite values.
Results may differ from the reference program's by a relative error of at most 0.0042.
Values may be sent and summed in bfloat16 or wider, within the bound.
No kernel may reach another device: no remote copies, remote signals or barrier semaphores. Data moves between devices by JAX's collectives and lax.ppermute only.
A program may use at most 128 MiB of HBM per device.

```python
import math
import jax
import jax.numpy as jnp
import numpy as np
from jax import lax

D = 6144
HEADS = 48
HEAD_DIM = 128
S = 128
MOSTF = 8
FRAMES = 128
CLIPS = 32
TOKENS = 16384


def draw_queries(key, part):
    key = jax.random.fold_in(key, 31)
    drawn = jnp.clip(1.6 * jax.random.normal(key, (TOKENS, D), jnp.float32), -8.0, 8.0)
    return drawn.astype(jnp.bfloat16)


def draw_keys(key, part):
    key = jax.random.fold_in(key, 32)
    drawn = jnp.clip(1.6 * jax.random.normal(key, (TOKENS, D), jnp.float32), -8.0, 8.0)
    return drawn.astype(jnp.bfloat16)


def draw_residual(key, part):
    key = jax.random.fold_in(key, 33)
    key_rows, key_cols, key_noise = jax.random.split(key, 3)
    row_level = jax.random.uniform(key_rows, (TOKENS, 1), jnp.float32)
    col_level = jax.random.uniform(key_cols, (1, D), jnp.float32)
    position = jnp.arange(D, dtype=jnp.float32)[None, :] / D
    scales = 10.0 ** (row_level + 0.5 * position + 0.5 * col_level - 1.0)
    pattern = jnp.clip(jax.random.normal(key_noise, (TOKENS, D), jnp.float32), -4.0, 4.0)
    return (scales * pattern).astype(jnp.bfloat16)


def draw_patch_counts(key, part):
    key = jax.random.fold_in(key, 34)
    key_grid, key_full = jax.random.split(key)
    counts = jax.random.randint(key_grid, (CLIPS,), S // 4, S + 1)
    widest = jax.random.randint(key_full, (), 0, CLIPS)
    return jnp.where(jnp.arange(CLIPS, dtype=jnp.int32) == widest, S, counts).astype(jnp.int32)


def level_of(stream_key, dims, cuts, smallest, largest):
    def one(dim, parts):
        draws = jax.random.uniform(jax.random.fold_in(jax.random.fold_in(stream_key, 6), dim), (parts,), jnp.float32, smallest / len(cuts), largest / len(cuts))
        return jnp.repeat(jnp.exp(draws), dims[dim] // parts).reshape((-1,) + (1,) * (len(dims) - dim - 1))

    level = one(*cuts[0])
    for cut in cuts[1:]:
        level = level * one(*cut)
    return level


def split_up(number_of, total, bound, lean):
    portions = [(1 << 20) // math.isqrt(standing ** lean) + 1 for standing in range(2, number_of + 1)]
    rest, given = total - bound - (number_of - 1), [1] * (number_of - 1)
    while rest > 0:
        candidates = [i for i in range(number_of - 1) if given[i] < bound]
        mass, left = sum([portions[i] for i in candidates]), rest
        for i in candidates:
            extra = min(bound - given[i], max(1, left * portions[i] // mass), rest)
            given[i] = given[i] + extra
            rest = rest - extra
    return np.array([bound] + given)


def ragged_sizes(rng, count, total, limit, lean):
    if count == 2:
        one = jax.random.randint(rng, (), max(1, total - limit), min(limit, total - 1) + 1)
        return jnp.stack([one, total - one])
    tallies = jnp.asarray(split_up(count, total, limit, lean), jnp.int32)
    twos = (count - 1) // 2
    source_of, sink = tallies[1:1 + 2 * twos:2], tallies[2:2 + 2 * twos:2]
    room = jnp.minimum(source_of - 1, limit - sink)
    shifted = jax.random.randint(jax.random.fold_in(rng, 1), (twos,), 0, 1 << 20) % (room + 1)
    tallies = tallies.at[1:1 + 2 * twos:2].set(source_of - shifted).at[2:2 + 2 * twos:2].set(sink + shifted)
    return tallies[jax.random.permutation(jax.random.fold_in(rng, 2), count)]


def gaussian(key, extent, spread, bound, cuts=(), held_as=jnp.bfloat16):
    gain = level_of(key, extent, cuts, -0.22, 0.18) if cuts else 1.0
    values = jax.random.normal(key, extent, jnp.float32) * spread * gain
    return jnp.minimum(jnp.maximum(values, -bound), bound).astype(held_as)


def setup_inputs(seed: int = 0) -> dict:
    streams_of = jax.random.split(jax.random.key(seed), 11)
    queries = draw_queries(jax.random.fold_in(streams_of[10], 71), 0)
    keys = draw_keys(jax.random.fold_in(streams_of[10], 71), 0)
    values = gaussian(streams_of[2], (TOKENS, D), 2.0, 10.0, ((0, 32), (1, 8)))
    residual = draw_residual(jax.random.fold_in(streams_of[10], 71), 0)
    out_weight = gaussian(streams_of[4], (D, D), D ** -0.5, 0.078125, ((0, 8), (1, 32)))
    gate = gaussian(streams_of[5], (CLIPS, D), 1.0, 4.0, ((1, 8),))
    mod_scale = gaussian(streams_of[6], (CLIPS, D), 0.5, 2.5, ((1, 8),))
    mod_shift = gaussian(streams_of[7], (CLIPS, D), 1.0, 4.0, ((1, 8),))
    frame_counts = ragged_sizes(streams_of[8], CLIPS, FRAMES, MOSTF, 2).astype(jnp.int32)
    patch_counts = draw_patch_counts(jax.random.fold_in(streams_of[10], 71), 0)
    return dict(queries=queries, keys=keys, values=values, residual=residual, out_weight=out_weight, gate=gate, mod_scale=mod_scale, mod_shift=mod_shift, frame_counts=frame_counts, patch_counts=patch_counts)


eps = 1e-06
negative = -1e+30

def clip_index(frame_counts, frame_ids):
    ends = jnp.cumsum(frame_counts)
    return lax.optimization_barrier(jnp.sum((ends[None, :] <= frame_ids[:, None]).astype(jnp.int32), axis=1)).astype(jnp.int32)

def softmax_rows(scores, key_mask):
    scores = jnp.where(key_mask, scores, negative)
    highest = lax.optimization_barrier(jnp.max(scores, axis=-1, keepdims=True))
    raised = jnp.exp(scores - highest)
    return (raised / lax.optimization_barrier(jnp.sum(raised, axis=-1, keepdims=True))).astype(jnp.bfloat16)

def reference(queries, keys, values, residual, out_weight, gate, mod_scale, mod_shift, frame_counts, patch_counts):
    frame_ids = jnp.arange(FRAMES, dtype=jnp.int32)
    clip_ids = clip_index(frame_counts, frame_ids)
    patch_grid = jnp.take(patch_counts, clip_ids, axis=0)
    live_cells = jnp.arange(S, dtype=jnp.int32)[None, :] < patch_grid[:, None]
    same_clip = clip_ids[:, None] == clip_ids[None, :]
    inv_scale = 1.0 / math.sqrt(HEAD_DIM)

    def by_pair(array):
        return jnp.moveaxis(array.reshape(FRAMES, S, HEADS // 2, 2, HEAD_DIM), 2, 0)

    def one_pair(triple):
        q_pair, k_pair, v_pair = triple
        q_space = q_pair[:, :, 0, :].astype(jnp.float32)
        k_space = k_pair[:, :, 0, :].astype(jnp.float32)
        v_space = v_pair[:, :, 0, :].astype(jnp.float32)
        q_time = q_pair[:, :, 1, :].astype(jnp.float32)
        k_time = k_pair[:, :, 1, :].astype(jnp.float32)
        v_time = v_pair[:, :, 1, :].astype(jnp.float32)
        space_scores = jnp.einsum('fpd,fqd->fpq', q_space, k_space) * inv_scale
        space_w = lax.optimization_barrier(softmax_rows(space_scores, live_cells[:, None, :]))
        space_out = jnp.einsum('fpq,fqd->fpd', space_w.astype(jnp.float32), v_space)
        space_out = jnp.where(live_cells[:, :, None], space_out, 0.0).astype(jnp.bfloat16)
        time_scores = jnp.einsum('fpd,gpd->pfg', q_time, k_time) * inv_scale
        time_mask = same_clip[None, :, :] & live_cells.T[:, None, :]
        time_w = lax.optimization_barrier(softmax_rows(time_scores, time_mask))
        time_out = jnp.einsum('pfg,gpd->fpd', time_w.astype(jnp.float32), v_time)
        time_out = jnp.where(live_cells[:, :, None], time_out, 0.0).astype(jnp.bfloat16)
        return jnp.stack([space_out, time_out], axis=2)
    pair_outs = lax.map(one_pair, (by_pair(queries), by_pair(keys), by_pair(values)))
    attended = jnp.moveaxis(pair_outs, 0, 2).reshape(TOKENS, D)
    proj = jnp.dot(attended, out_weight, preferred_element_type=jnp.float32)
    gate_frames = jnp.take(gate, clip_ids, axis=0).astype(jnp.float32)
    scale_frames = jnp.take(mod_scale, clip_ids, axis=0).astype(jnp.float32)
    shift_frames = jnp.take(mod_shift, clip_ids, axis=0).astype(jnp.float32)
    combined = residual.astype(jnp.float32).reshape(FRAMES, S, D) + gate_frames[:, None, :] * proj.reshape(FRAMES, S, D)
    updated = lax.optimization_barrier(combined.astype(jnp.bfloat16))
    widened = updated.astype(jnp.float32)
    mean_sq = lax.optimization_barrier(jnp.mean(widened * widened, axis=2, keepdims=True))
    normed = widened * lax.rsqrt(mean_sq + eps) * (1.0 + scale_frames[:, None, :]) + shift_frames[:, None, :]
    return (updated.reshape(TOKENS, D), normed.astype(jnp.bfloat16).reshape(TOKENS, D))
```

```python
import functools
import math

import jax
import jax.numpy as jnp
from jax import lax
from jax.experimental import pallas as pl
from jax.experimental.pallas import tpu as pltpu
from jax.sharding import PartitionSpec as P

D = 6144
HD = 128
S = 128
FR = 4
X, Y, Z, CORES = 4, 4, 8, 2
ROWS = FR * S
COLS = D // (X * CORES)
HALF = COLS // 2
WB = D // (Y * Z)
GROUP = 16
eps = 1e-06
negative = -1e30
NT = (((1,), (1,)), ((), ()))
VM = 60 * 1024 * 1024


def seq_perm(dy, dz):
    return [
        (y * Z + z, (y + dy) % Y * Z + (z + dz) % Z) for y in range(Y) for z in range(Z)
    ]


def ring_perm(d):
    n = Y * Z
    return [(i, (i + d) % n) for i in range(n)]


def mp_perm(dx, dc):
    return [
        (x * CORES + c, (x + dx) % X * CORES + (c + dc) % CORES)
        for x in range(X)
        for c in range(CORES)
    ]


def swap_perm():
    pairs = []
    for x in range(X):
        for y in range(Y):
            for z in range(Z):
                for c in range(CORES):
                    src = (y * Z + z) * X * CORES + x * CORES + c
                    dst = (x * Z + z) * X * CORES + y * CORES + c
                    pairs.append((src, dst))
    return pairs


def seq_move(a, dy, dz):
    return lax.ppermute(a, "seq", seq_perm(dy, dz))


def mp_move(a, dx, dc=0):
    return lax.ppermute(a, "mp", mp_perm(dx, dc))


def clip_index(frame_counts, frame_ids):
    ends = jnp.cumsum(frame_counts)
    return jnp.sum((ends[None, :] <= frame_ids[:, None]).astype(jnp.int32), axis=1)


def cost(flops, nbytes):
    return pl.CostEstimate(flops=flops, bytes_accessed=nbytes, transcendentals=0)


def pack_kv_kernel(k_ref, v_ref, o_ref):
    o_ref[0] = k_ref[...]
    o_ref[1] = v_ref[...]


def pack_kv(keys, values):
    return pl.pallas_call(
        pack_kv_kernel,
        grid=(3,),
        in_specs=[pl.BlockSpec((ROWS, HD), lambda j: (0, 2 * j + 1))] * 2,
        out_specs=pl.BlockSpec((2, ROWS, HD), lambda j: (0, 0, j)),
        out_shape=jax.ShapeDtypeStruct((2, ROWS, HALF), jnp.bfloat16),
        cost_estimate=cost(0, 4 * ROWS * HALF * 2),
        name="pack_kv",
    )(keys, values)


def pack_w_kernel(w_ref, o_ref):
    for j in range(COLS // HD):
        at = (j // 2) * HD + (j % 2) * HALF
        o_ref[:, at : at + HD] = w_ref[j * HD : (j + 1) * HD, :].T


def pack_w(weight):
    return pl.pallas_call(
        pack_w_kernel,
        out_shape=jax.ShapeDtypeStruct((WB, COLS), jnp.bfloat16),
        cost_estimate=cost(0, 2 * WB * COLS * 2),
        name="pack_w",
    )(weight)


def softmax_weights(scores):
    highest = jnp.max(scores, axis=-1, keepdims=True)
    raised = jnp.exp(scores - highest)
    return (raised / jnp.sum(raised, axis=-1, keepdims=True)).astype(jnp.bfloat16)


def even_kernel(grid_ref, q_ref, k_ref, v_ref, o_ref):
    count = grid_ref[pl.program_id(0)]
    key_live = lax.broadcasted_iota(jnp.int32, (S, S), 1) < count
    row_live = lax.broadcasted_iota(jnp.int32, (S, HD), 0) < count
    for h in range(3):
        at = slice(2 * h * HD, (2 * h + 1) * HD)
        scores = lax.dot_general(
            q_ref[:, at], k_ref[:, at], NT, preferred_element_type=jnp.float32
        ) * (1.0 / math.sqrt(HD))
        weights = softmax_weights(jnp.where(key_live, scores, negative))
        out = jnp.dot(weights, v_ref[:, at], preferred_element_type=jnp.float32)
        o_ref[:, h * HD : (h + 1) * HD] = jnp.where(row_live, out, 0.0).astype(jnp.bfloat16)


def even_attention(own_grid, queries, keys, values):
    block = pl.BlockSpec((S, COLS), lambda f, g: (f, 0))
    return pl.pallas_call(
        even_kernel,
        grid_spec=pltpu.PrefetchScalarGridSpec(
            num_scalar_prefetch=1,
            grid=(FR,),
            in_specs=[block] * 3,
            out_specs=pl.BlockSpec((S, HALF), lambda f, g: (f, 0)),
        ),
        out_shape=jax.ShapeDtypeStruct((ROWS, HALF), jnp.bfloat16),
        cost_estimate=cost(FR * 3 * 4 * S * S * HD, 4 * ROWS * COLS * 2),
        name="even_attention",
    )(own_grid, queries, keys, values)


WINDOW = 18


def odd_kernel(grid_ref, mask_ref, q_ref, k_ref, v_ref, l1_ref, r1_ref, l2_ref, r2_ref, o_ref):
    base = pl.program_id(0) * GROUP
    allowed = mask_ref[...] > 0.5
    cell = base + lax.broadcasted_iota(jnp.int32, (GROUP, HD), 0)
    for h in range(3):
        wide = slice((2 * h + 1) * HD, (2 * h + 2) * HD)
        at = slice(h * HD, (h + 1) * HD)

        def window(own_ref, which):
            parts = [
                own_ref[:, :, wide],
                l1_ref[which, :, :, at],
                r1_ref[which, :, :, at],
                l2_ref[which, :, :, at],
                r2_ref[which, :, :, at],
            ]
            return jnp.concatenate([p.reshape(-1, HD) for p in parts], axis=0)

        q = q_ref[:, :, wide].reshape(FR * GROUP, HD)
        scores = lax.dot_general(
            q, window(k_ref, 0), NT, preferred_element_type=jnp.float32
        ) * (1.0 / math.sqrt(HD))
        weights = softmax_weights(jnp.where(allowed, scores, negative))
        out = jnp.dot(weights, window(v_ref, 1), preferred_element_type=jnp.float32)
        for f in range(FR):
            part = jnp.where(cell < grid_ref[f], out[f * GROUP : (f + 1) * GROUP], 0.0)
            o_ref[f, :, at] = part.astype(jnp.bfloat16)


def odd_attention(own_grid, mask, queries, keys, values, left1, right1, left2, right2):
    def frames(a):
        return a.reshape(FR, S, COLS)

    own = pl.BlockSpec((FR, GROUP, COLS), lambda i, g: (0, i, 0))
    near = pl.BlockSpec((2, FR, GROUP, HALF), lambda i, g: (0, 0, i, 0))
    far = pl.BlockSpec((2, FR - 1, GROUP, HALF), lambda i, g: (0, 0, i, 0))
    out = pl.pallas_call(
        odd_kernel,
        grid_spec=pltpu.PrefetchScalarGridSpec(
            num_scalar_prefetch=1,
            grid=(S // GROUP,),
            in_specs=[
                pl.BlockSpec((FR * GROUP, WINDOW * GROUP), lambda i, g: (0, 0)),
                own,
                own,
                own,
                near,
                near,
                far,
                far,
            ],
            out_specs=pl.BlockSpec((FR, GROUP, HALF), lambda i, g: (0, i, 0)),
        ),
        out_shape=jax.ShapeDtypeStruct((FR, S, HALF), jnp.bfloat16),
        cost_estimate=cost(ROWS * 3 * 4 * WINDOW * GROUP * HD, 10 * ROWS * COLS * 2),
        name="odd_attention",
    )(own_grid, mask, frames(queries), frames(keys), frames(values), left1, right1, left2, right2)
    return out.reshape(ROWS, HALF)


def project_kernel(w_places, out_type, place_ref, *refs):
    a_refs = refs[:8]
    w_refs = refs[8 : 8 + len(w_places)]
    o_ref, a_buf, w_buf, acc, a_sem, w_sem = refs[8 + len(w_places) :]
    x, y, z, half = place_ref[0], place_ref[1], place_ref[2], place_ref[3]
    for r in range(X):
        slot = lax.rem(x + r, X)
        for part in range(2):
            pltpu.make_async_copy(
                a_refs[2 * r + part],
                a_buf.at[slot, :, part * HALF : (part + 1) * HALF],
                a_sem.at[slot],
            ).start()
    for ref, blocks in zip(w_refs, w_places):
        start = 0
        for dy, dz, first, rows in blocks:
            slot = lax.rem(y + dy + Y, Y)
            column = lax.rem(z + dz + Z, Z)
            at = pl.multiple_of(lax.rem(column, Z // 2) * WB + first, 32)
            source = ref.at[start : start + rows]

            @pl.when(column // (Z // 2) == half)
            def _(source=source, slot=slot, at=at, rows=rows):
                pltpu.make_async_copy(
                    source, w_buf.at[slot, pl.ds(at, rows)], w_sem.at[slot]
                ).start()

            start += rows
    acc[...] = jnp.zeros_like(acc)

    @pl.loop(0, Y)
    def _(j):
        pltpu.make_async_copy(a_buf.at[j], a_buf.at[j], a_sem.at[j]).wait()
        pltpu.make_async_copy(w_buf.at[j], w_buf.at[j], w_sem.at[j]).wait()
        acc[...] += lax.dot_general(
            a_buf[j], w_buf[j], NT, preferred_element_type=jnp.float32
        )

    o_ref[...] = acc[...].astype(out_type)


def project(place, a_parts, w_parts, w_places, out_type):
    hbm = pl.BlockSpec(memory_space=pl.ANY)
    return pl.pallas_call(
        functools.partial(project_kernel, w_places, out_type),
        grid_spec=pltpu.PrefetchScalarGridSpec(
            num_scalar_prefetch=1,
            grid=(1,),
            in_specs=[hbm] * (len(a_parts) + len(w_parts)),
            out_specs=pl.BlockSpec((ROWS, COLS), lambda i, p: (0, 0)),
            scratch_shapes=[
                pltpu.VMEM((X, ROWS, COLS), jnp.bfloat16),
                pltpu.VMEM((Y, COLS, COLS), jnp.bfloat16),
                pltpu.VMEM((ROWS, COLS), jnp.float32),
                pltpu.SemaphoreType.DMA((X,)),
                pltpu.SemaphoreType.DMA((Y,)),
            ],
        ),
        out_shape=jax.ShapeDtypeStruct((ROWS, COLS), out_type),
        compiler_params=pltpu.CompilerParams(vmem_limit_bytes=32 * 1024 * 1024),
        cost_estimate=cost(2 * ROWS * COLS * COLS * 4, 9 * 1024 * 1024),
        name="project",
    )(place, *a_parts, *w_parts)


def update_kernel(own_ref, other_ref, residual_ref, gate_ref, u_ref, sq_ref):
    total = own_ref[...] + other_ref[...].astype(jnp.float32)
    combined = residual_ref[...].astype(jnp.float32) + gate_ref[0] * total
    updated = combined.astype(jnp.bfloat16)
    u_ref[...] = updated
    wide = updated.astype(jnp.float32)
    squares = wide * wide
    folded = squares[:, :HD]
    for j in range(1, COLS // HD):
        folded = folded + squares[:, j * HD : (j + 1) * HD]
    sq_ref[0] = jnp.sum(folded.T, axis=0, keepdims=True)


def update(own, other, residual, gate_rows):
    block = pl.BlockSpec((S, COLS), lambda f: (f, 0))
    return pl.pallas_call(
        update_kernel,
        grid=(FR,),
        in_specs=[block, block, block, pl.BlockSpec((1, 1, COLS), lambda f: (f, 0, 0))],
        out_specs=[block, pl.BlockSpec((1, 1, S), lambda f: (f, 0, 0))],
        out_shape=[
            jax.ShapeDtypeStruct((ROWS, COLS), jnp.bfloat16),
            jax.ShapeDtypeStruct((FR, 1, S), jnp.float32),
        ],
        cost_estimate=cost(0, ROWS * COLS * 10),
        name="update",
    )(own, other, residual, gate_rows)


def norm_kernel(u_ref, s0_ref, s1_ref, s2_ref, s3_ref, scale_ref, shift_ref, o_ref):
    total = s0_ref[0] + s1_ref[0] + s2_ref[0] + s3_ref[0]
    inverse = lax.rsqrt(total * (1.0 / D) + eps)
    inverse = jnp.broadcast_to(inverse, (S, S)).T
    for j in range(COLS // HD):
        at = slice(j * HD, (j + 1) * HD)
        wide = u_ref[:, at].astype(jnp.float32)
        normed = wide * inverse * (1.0 + scale_ref[0, :, at]) + shift_ref[0, :, at]
        o_ref[:, at] = normed.astype(jnp.bfloat16)


def norm(updated, sums, scale_rows, shift_rows):
    block = pl.BlockSpec((S, COLS), lambda f: (f, 0))
    row = pl.BlockSpec((1, 1, COLS), lambda f: (f, 0, 0))
    lane = pl.BlockSpec((1, 1, S), lambda f: (f, 0, 0))
    return pl.pallas_call(
        norm_kernel,
        grid=(FR,),
        in_specs=[block, lane, lane, lane, lane, row, row],
        out_specs=block,
        out_shape=jax.ShapeDtypeStruct((ROWS, COLS), jnp.bfloat16),
        cost_estimate=cost(0, ROWS * COLS * 4),
        name="norm",
    )(updated, *sums, scale_rows, shift_rows)


def gather_weight(weight):
    parts, places = [], []

    def keep(a, *blocks):
        parts.append(a)
        places.append(tuple(blocks))

    def whole(dy, dz):
        return (dy, dz, 0, WB)

    own = lax.ppermute(pack_w(weight), ("seq", "mp"), swap_perm())
    far = seq_move(own, 2, 0)
    pair = jnp.concatenate([own, far], axis=0)
    keep(pair, whole(0, 0), whole(2, 0))
    up, down = seq_move(own, 1, 0), seq_move(own, -1, 0)
    keep(up, whole(-1, 0))
    keep(down, whole(1, 0))
    right1, left1 = seq_move(pair, 0, 1), seq_move(pair, 0, -1)
    keep(right1, whole(0, -1), whole(2, -1))
    keep(left1, whole(0, 1), whole(2, 1))
    chunk = jnp.concatenate([right1[:WB], left1[:WB]], axis=0)
    up, down = seq_move(chunk, 1, 0), seq_move(chunk, -1, 0)
    keep(up, whole(-1, -1), whole(-1, 1))
    keep(down, whole(1, -1), whole(1, 1))
    right2, left2 = seq_move(right1, 0, 1), seq_move(left1, 0, -1)
    keep(right2, whole(0, -2), whole(2, -2))
    keep(left2, whole(0, 2), whole(2, 2))
    chunk = jnp.concatenate([right2[:WB], left2[:WB]], axis=0)
    up, down = seq_move(chunk, 1, 0), seq_move(chunk, -1, 0)
    keep(up, whole(-1, -2), whole(-1, 2))
    keep(down, whole(1, -2), whole(1, 2))
    right3, left3 = seq_move(right2[:WB], 0, 1), seq_move(left2[:WB], 0, -1)
    keep(right3, whole(0, -3))
    keep(left3, whole(0, 3))
    right4 = seq_move(right3, 0, 1)
    keep(right4, whole(0, -4))
    chunk = jnp.concatenate([right3, left3, right4], axis=0)
    up, down = seq_move(chunk, 1, 0), seq_move(chunk, -1, 0)
    keep(up, whole(-1, -3), whole(-1, 3), whole(-1, -4))
    keep(down, whole(1, -3), whole(1, 3), whole(1, -4))
    h = WB // 2
    first = jnp.concatenate([down[:WB], down[2 * WB : 2 * WB + h]], axis=0)
    second = jnp.concatenate([up[WB : 2 * WB], up[2 * WB + h :]], axis=0)
    keep(seq_move(first, -1, 0), whole(2, -3), (2, -4, 0, h))
    keep(seq_move(second, 1, 0), whole(2, 3), (2, -4, h, h))
    return parts, places


def gather_x(a):
    return [a, mp_move(a, -1), mp_move(a, 2), mp_move(a, 1)]


def local(
    queries,
    keys,
    values,
    residual,
    out_weight,
    gate,
    mod_scale,
    mod_shift,
    frame_counts,
    patch_counts,
):
    s = lax.axis_index("seq")
    m = lax.axis_index("mp")
    x, core = m // CORES, m % CORES
    y, z = s // Z, s % Z
    clip_total = frame_counts.shape[0]

    kv = pack_kv(keys, values).reshape(2, FR, S, HALF)
    from_left = lax.ppermute(kv, "seq", ring_perm(1))
    from_right = lax.ppermute(kv, "seq", ring_perm(-1))
    from_left2 = lax.ppermute(from_left[:, 1:], "seq", ring_perm(1))
    from_right2 = lax.ppermute(from_right[:, : FR - 1], "seq", ring_perm(-1))
    w_parts, w_places = gather_weight(out_weight)

    first = s * FR
    own_ids = first + jnp.arange(FR, dtype=jnp.int32)
    own_clips = clip_index(frame_counts, own_ids)
    hot = own_clips[:, None] == jnp.arange(clip_total, dtype=jnp.int32)[None, :]
    own_grid = jnp.sum(jnp.where(hot, patch_counts[None, :], 0), axis=1)
    rel = [0, 1, 2, 3, -4, -3, -2, -1, 4, 5, 6, 7, -7, -6, -5, 8, 9, 10]
    key_ids = first + jnp.array(rel, dtype=jnp.int32)
    inside = (key_ids >= 0) & (key_ids < FR * Y * Z)
    key_clips = jnp.where(inside, clip_index(frame_counts, key_ids), -1)
    same_clip = own_clips[:, None] == key_clips[None, :]
    cells = jnp.arange(GROUP, dtype=jnp.int32)
    mask = same_clip[:, None, :, None] & (cells[None, :, None, None] == cells[None, None, None, :])
    mask = mask.astype(jnp.float32).reshape(FR * GROUP, WINDOW * GROUP)

    even = even_attention(own_grid, queries, keys, values)
    even_parts = gather_x(even)
    odd = odd_attention(
        own_grid, mask, queries, keys, values, from_left, from_right, from_left2, from_right2
    )
    odd_parts = gather_x(odd)
    a_parts = [a for pair in zip(even_parts, odd_parts) for a in pair]

    other_place = jnp.stack([x, y, z, 1 - core]).astype(jnp.int32)
    own_place = jnp.stack([x, y, z, core]).astype(jnp.int32)
    other_half = project(other_place, a_parts, w_parts, w_places, jnp.bfloat16)
    swapped = mp_move(other_half, 0, 1)
    own_half = project(own_place, a_parts, w_parts, w_places, jnp.float32)

    hot = hot.astype(jnp.bfloat16)

    def lookup(table):
        rows = jnp.dot(hot, table, preferred_element_type=jnp.float32)
        return rows.reshape(FR, 1, COLS)

    updated, squares = update(own_half, swapped, residual, lookup(gate))
    squares = squares + mp_move(squares, 0, 1)
    sums = gather_x(squares)
    normed = norm(updated, sums, lookup(mod_scale), lookup(mod_shift))
    return updated, normed


def solution(mesh):
    in_specs = (
        P("seq", "mp"),
        P("seq", "mp"),
        P("seq", "mp"),
        P("seq", "mp"),
        P("mp", "seq"),
        P(None, "mp"),
        P(None, "mp"),
        P(None, "mp"),
        P(),
        P(),
    )
    out_specs = (P("seq", "mp"), P("seq", "mp"))
    return jax.shard_map(local, mesh=mesh, in_specs=in_specs, out_specs=out_specs, check_vma=False)
```

```python
import functools
import math

import jax
import jax.numpy as jnp
from jax import lax
from jax.experimental import pallas as pl
from jax.experimental.pallas import tpu as pltpu
from jax.sharding import PartitionSpec as P

D = 6144
HD = 128
S = 128
FR = 4
X, Y, Z, CORES = 4, 4, 8, 2
ROWS = FR * S
COLS = D // (X * CORES)
HALF = COLS // 2
WB = D // (Y * Z)
GROUP = 16
eps = 1e-06
negative = -1e30
NT = (((1,), (1,)), ((), ()))
HBM = pl.BlockSpec(memory_space=pltpu.HBM)
ROOM = pltpu.CompilerParams(vmem_limit_bytes=56 * 1024 * 1024)


def ring_perm(d):
    n = Y * Z
    return [(i, (i + d) % n) for i in range(n)]


def mp_perm(dx, dc):
    return [
        (x * CORES + c, (x + dx) % X * CORES + (c + dc) % CORES)
        for x in range(X)
        for c in range(CORES)
    ]


def device(x, y, z, c):
    return (y * Z + z) * X * CORES + x * CORES + c


PLACES = [(x, y, z, c) for x in range(X) for y in range(Y) for z in range(Z) for c in range(CORES)]


def weight_perm():
    half = Z // 2
    return [
        (device(x, y, z, c), device(y, x, z % half * CORES + c, z // half)) for x, y, z, c in PLACES
    ]


def spread_perm(shift):
    return [(device(x, y, z, c), device((y + shift) % X, x, z, c)) for x, y, z, c in PLACES]


def mp_move(a, dx, dc=0):
    return lax.ppermute(a, "mp", mp_perm(dx, dc))


def clip_index(frame_counts, frame_ids):
    ends = jnp.cumsum(frame_counts)
    return jnp.sum((ends[None, :] <= frame_ids[:, None]).astype(jnp.int32), axis=1)


def cost(flops, nbytes):
    return pl.CostEstimate(flops=flops, bytes_accessed=nbytes, transcendentals=0)


def pack_kv_kernel(k_ref, v_ref, r3_ref, r1_ref, l3_ref, l1_ref):
    for which, ref in enumerate((k_ref, v_ref)):
        r3_ref[which] = ref[1:]
        r1_ref[which] = ref[:1]
        l3_ref[which] = ref[: FR - 1]
        l1_ref[which] = ref[FR - 1 :]


def pack_kv(keys, values):
    sizes = (FR - 1, 1, FR - 1, 1)
    return pl.pallas_call(
        pack_kv_kernel,
        grid=(3,),
        in_specs=[pl.BlockSpec((FR, S, HD), lambda j: (0, 0, 2 * j + 1))] * 2,
        out_specs=[pl.BlockSpec((2, n, S, HD), lambda j: (0, 0, 0, j)) for n in sizes],
        out_shape=[jax.ShapeDtypeStruct((2, n, S, HALF), jnp.bfloat16) for n in sizes],
        compiler_params=ROOM,
        cost_estimate=cost(0, 6 * ROWS * HALF * 2),
        name="pack_kv",
    )(keys.reshape(FR, S, COLS), values.reshape(FR, S, COLS))


def softmax_weights(scores):
    highest = jnp.max(scores, axis=-1, keepdims=True)
    raised = jnp.exp(scores - highest)
    inverse = 1.0 / jnp.sum(raised, axis=-1, keepdims=True)
    return (raised * inverse).astype(jnp.bfloat16)


EVEN_FRAMES = 2


def even_kernel(info_ref, q_ref, k_ref, v_ref, o_ref):
    base = pl.program_id(0) * EVEN_FRAMES
    lane = lax.broadcasted_iota(jnp.int32, (S, S), 1)
    row = lax.broadcasted_iota(jnp.int32, (S, HD), 0)
    pieces = [(f, h) for f in range(EVEN_FRAMES) for h in range(3)]

    def take(ref, f, h):
        return ref[f * S : (f + 1) * S, 2 * h * HD : (2 * h + 1) * HD]

    scores = []
    for f, h in pieces:
        raw = lax.dot_general(
            take(q_ref, f, h), take(k_ref, f, h), NT, preferred_element_type=jnp.float32
        ) * (1.0 / math.sqrt(HD))
        scores.append(jnp.where(lane < info_ref[FR + base + f], raw, negative))
    weights = softmax_weights(jnp.concatenate(scores, axis=0))
    for i, (f, h) in enumerate(pieces):
        out = jnp.dot(
            weights[i * S : (i + 1) * S], take(v_ref, f, h), preferred_element_type=jnp.float32
        )
        out = jnp.where(row < info_ref[FR + base + f], out, 0.0).astype(jnp.bfloat16)
        o_ref[f * S : (f + 1) * S, h * HD : (h + 1) * HD] = out


def even_attention(info, queries, keys, values):
    block = pl.BlockSpec((EVEN_FRAMES * S, COLS), lambda f, g: (f, 0))
    return pl.pallas_call(
        even_kernel,
        grid_spec=pltpu.PrefetchScalarGridSpec(
            num_scalar_prefetch=1,
            grid=(FR // EVEN_FRAMES,),
            in_specs=[block] * 3,
            out_specs=pl.BlockSpec((EVEN_FRAMES * S, HALF), lambda f, g: (f, 0)),
        ),
        out_shape=jax.ShapeDtypeStruct((ROWS, HALF), jnp.bfloat16),
        compiler_params=ROOM,
        cost_estimate=cost(FR * 3 * 4 * S * S * HD, 4 * ROWS * COLS * 2),
        name="even_attention",
    )(info, queries, keys, values)


WINDOW = 18
BATCH = 2


def odd_kernel(info_ref, clip_ref, q_ref, k_ref, v_ref, *refs):
    far_refs, o_ref = refs[:-1], refs[-1]
    keys_wide = WINDOW * GROUP
    query_cell = lax.broadcasted_iota(jnp.int32, (GROUP, keys_wide), 0)
    key_cell = lax.rem(lax.broadcasted_iota(jnp.int32, (GROUP, keys_wide), 1), GROUP)
    same_cell = query_cell == key_cell
    allowed = [same_cell & (clip_ref[...] == info_ref[f]) for f in range(FR)]
    cell = lax.broadcasted_iota(jnp.int32, (GROUP, HD), 0)
    pieces = [(b, h) for b in range(BATCH) for h in range(3)]

    def window(own_ref, which, b, h):
        rows = slice(b * GROUP, (b + 1) * GROUP)
        wide = slice((2 * h + 1) * HD, (2 * h + 2) * HD)
        at = slice(h * HD, (h + 1) * HD)
        parts = [own_ref[:, rows, wide]]
        parts += [r[which, :, rows, at] for r in far_refs]
        return jnp.concatenate([p.reshape(-1, HD) for p in parts], axis=0)

    scores = []
    for b, h in pieces:
        q = q_ref[:, b * GROUP : (b + 1) * GROUP, (2 * h + 1) * HD : (2 * h + 2) * HD]
        raw = lax.dot_general(
            q.reshape(FR * GROUP, HD), window(k_ref, 0, b, h), NT,
            preferred_element_type=jnp.float32,
        ) * (1.0 / math.sqrt(HD))
        for f in range(FR):
            scores.append(jnp.where(allowed[f], raw[f * GROUP : (f + 1) * GROUP], negative))
    weights = softmax_weights(jnp.concatenate(scores, axis=0))
    n = FR * GROUP
    for i, (b, h) in enumerate(pieces):
        out = jnp.dot(
            weights[i * n : (i + 1) * n], window(v_ref, 1, b, h),
            preferred_element_type=jnp.float32,
        )
        first = (pl.program_id(0) * BATCH + b) * GROUP
        for f in range(FR):
            part = out[f * GROUP : (f + 1) * GROUP]
            part = jnp.where(first + cell < info_ref[FR + f], part, 0.0)
            o_ref[f, b * GROUP : (b + 1) * GROUP, h * HD : (h + 1) * HD] = part.astype(
                jnp.bfloat16
            )


def odd_attention(info, key_clips, queries, keys, values, others):
    def frames(a):
        return a.reshape(FR, S, COLS)

    step = GROUP * BATCH
    own = pl.BlockSpec((FR, step, COLS), lambda i, g: (0, i, 0))

    def other(n):
        return pl.BlockSpec((2, n, step, HALF), lambda i, g: (0, 0, i, 0))

    out = pl.pallas_call(
        odd_kernel,
        grid_spec=pltpu.PrefetchScalarGridSpec(
            num_scalar_prefetch=1,
            grid=(S // step,),
            in_specs=[
                pl.BlockSpec((1, WINDOW * GROUP), lambda i, g: (0, 0)),
                own, own, own, *[other(a.shape[1]) for a in others],
            ],
            out_specs=pl.BlockSpec((FR, step, HALF), lambda i, g: (0, i, 0)),
        ),
        out_shape=jax.ShapeDtypeStruct((FR, S, HALF), jnp.bfloat16),
        compiler_params=ROOM,
        cost_estimate=cost(ROWS * 3 * 4 * WINDOW * GROUP * HD, 10 * ROWS * COLS * 2),
        name="odd_attention",
    )(info, key_clips, frames(queries), frames(keys), frames(values), *others)
    return out.reshape(ROWS, HALF)


def project_kernel(shifts, info_ref, *refs):
    own_refs, other_even, other_odd = refs[: 2 * X], refs[2 * X], refs[2 * X + 1 : 3 * X + 1]
    w_ref = refs[3 * X + 1]
    n = len(shifts)
    o_refs, (a_buf, w_buf, a_sem, w_sem) = refs[3 * X + 2 : 3 * X + 2 + n], refs[3 * X + 2 + n :]
    x, y, core = info_ref[2 * FR], info_ref[2 * FR + 1], info_ref[2 * FR + 2]
    half = Z // 2
    w_copies = [
        pltpu.make_async_copy(
            w_ref.at[CORES * i + c], w_buf.at[i, :, c * COLS : (c + 1) * COLS], w_sem.at[i]
        )
        for i in range(half)
        for c in range(CORES)
    ]
    for copy in w_copies:
        copy.start()
    for i, d in enumerate(shifts):
        slot = lax.rem(x - y - d + 2 * X, X)
        for r in range(X):
            sources = [own_refs[2 * r], own_refs[2 * r + 1]]
            sources += [other_even.at[r * ROWS : (r + 1) * ROWS], other_odd[r]]

            @pl.when(slot == r)
            def _(sources=sources, i=i):
                for k, source in enumerate(sources):
                    side = core if k < 2 else 1 - core
                    for h in range(3):
                        at = pl.multiple_of(side * COLS + (2 * h + k % 2) * HD, HD)
                        pltpu.make_async_copy(
                            source.at[:, h * HD : (h + 1) * HD],
                            a_buf.at[i, :, pl.ds(at, HD)],
                            a_sem.at[i],
                        ).start()
    for copy in w_copies:
        copy.wait()
    for i in range(n):
        pltpu.make_async_copy(a_buf.at[i], a_buf.at[i], a_sem.at[i]).wait()
        total = lax.dot_general(
            a_buf[i], w_buf[...].reshape(COLS, 2 * COLS), NT, preferred_element_type=jnp.float32
        )
        o_refs[i][...] = total.astype(o_refs[i].dtype)


def project(info, operands, shifts, out_type):
    n = len(shifts)
    return pl.pallas_call(
        functools.partial(project_kernel, shifts),
        grid_spec=pltpu.PrefetchScalarGridSpec(
            num_scalar_prefetch=1,
            grid=(1,),
            in_specs=[HBM] * len(operands),
            out_specs=[pl.BlockSpec((ROWS, COLS), lambda i, p: (0, 0))] * n,
            scratch_shapes=[
                pltpu.VMEM((n, ROWS, 2 * COLS), jnp.bfloat16),
                pltpu.VMEM((Z // 2, WB, 2 * COLS), jnp.bfloat16),
                pltpu.SemaphoreType.DMA((n,)),
                pltpu.SemaphoreType.DMA((Z // 2,)),
            ],
        ),
        out_shape=[jax.ShapeDtypeStruct((ROWS, COLS), out_type)] * n,
        compiler_params=ROOM,
        cost_estimate=cost(4 * n * ROWS * COLS * COLS, 4 * 1024 * 1024),
        name="project",
    )(info, *operands)


TAIL_FRAMES = 2


def table_row(table_ref, clip):
    lane = lax.broadcasted_iota(jnp.int32, (8, table_ref.shape[0]), 1)
    hot = jnp.where(lane == clip, 1.0, 0.0).astype(jnp.bfloat16)
    return jnp.dot(hot, table_ref[...], preferred_element_type=jnp.float32)[:1]


def update_kernel(
    info_ref, own_ref, p0_ref, p1_ref, p2_ref, residual_ref, gate_ref, u_ref, sq_ref
):
    for f in range(TAIL_FRAMES):
        rows = slice(f * S, (f + 1) * S)
        gate = table_row(gate_ref, info_ref[pl.program_id(0) * TAIL_FRAMES + f])
        folded = None
        for j in range(COLS // HD):
            at = slice(j * HD, (j + 1) * HD)
            total = own_ref[rows, at]
            for part_ref in (p0_ref, p1_ref, p2_ref):
                total = total + part_ref[rows, at].astype(jnp.float32)
            combined = residual_ref[rows, at].astype(jnp.float32) + gate[:, at] * total
            updated = combined.astype(jnp.bfloat16)
            u_ref[rows, at] = updated
            wide = updated.astype(jnp.float32)
            folded = wide * wide if folded is None else folded + wide * wide
        sq_ref[f] = jnp.sum(folded.T, axis=0, keepdims=True)


def update(info, own, parts, residual, gate):
    block = pl.BlockSpec((TAIL_FRAMES * S, COLS), lambda f, g: (f, 0))
    return pl.pallas_call(
        update_kernel,
        grid_spec=pltpu.PrefetchScalarGridSpec(
            num_scalar_prefetch=1,
            grid=(FR // TAIL_FRAMES,),
            in_specs=[block] * 5 + [pl.BlockSpec(gate.shape, lambda f, g: (0, 0))],
            out_specs=[block, pl.BlockSpec((TAIL_FRAMES, 1, S), lambda f, g: (f, 0, 0))],
        ),
        out_shape=[
            jax.ShapeDtypeStruct((ROWS, COLS), jnp.bfloat16),
            jax.ShapeDtypeStruct((FR, 1, S), jnp.float32),
        ],
        compiler_params=ROOM,
        cost_estimate=cost(0, ROWS * COLS * 14),
        name="update",
    )(info, own, *parts, residual, gate)


def norm_kernel(info_ref, u_ref, s0_ref, s1_ref, s2_ref, s3_ref, scale_ref, shift_ref, o_ref):
    for f in range(TAIL_FRAMES):
        rows = slice(f * S, (f + 1) * S)
        clip = info_ref[pl.program_id(0) * TAIL_FRAMES + f]
        scale, shift = table_row(scale_ref, clip), table_row(shift_ref, clip)
        total = s0_ref[f] + s1_ref[f] + s2_ref[f] + s3_ref[f]
        inverse = lax.rsqrt(total * (1.0 / D) + eps)
        inverse = jnp.broadcast_to(inverse, (S, S)).T
        for j in range(COLS // HD):
            at = slice(j * HD, (j + 1) * HD)
            wide = u_ref[rows, at].astype(jnp.float32)
            normed = wide * inverse * (1.0 + scale[:, at]) + shift[:, at]
            o_ref[rows, at] = normed.astype(jnp.bfloat16)


def norm(info, updated, sums, scale, shift):
    block = pl.BlockSpec((TAIL_FRAMES * S, COLS), lambda f, g: (f, 0))
    table = pl.BlockSpec(scale.shape, lambda f, g: (0, 0))
    lane = pl.BlockSpec((TAIL_FRAMES, 1, S), lambda f, g: (f, 0, 0))
    return pl.pallas_call(
        norm_kernel,
        grid_spec=pltpu.PrefetchScalarGridSpec(
            num_scalar_prefetch=1,
            grid=(FR // TAIL_FRAMES,),
            in_specs=[block, lane, lane, lane, lane, table, table],
            out_specs=block,
        ),
        out_shape=jax.ShapeDtypeStruct((ROWS, COLS), jnp.bfloat16),
        compiler_params=ROOM,
        cost_estimate=cost(0, ROWS * COLS * 4),
        name="norm",
    )(info, updated, *sums, scale, shift)


def gather_weight(own):
    groups = [[y * Z + z for z in range(Z)] for y in range(Y)]
    return lax.all_gather(own, "seq", axis=0, tiled=False, axis_index_groups=groups)


def spread(a):
    return [lax.ppermute(a, ("seq", "mp"), spread_perm(r)) for r in range(X)]


def gather_x(a):
    return [a, mp_move(a, -1), mp_move(a, 2), mp_move(a, 1)]


def seq_move(a, dy):
    perm = [(y * Z + z, (y + dy) % Y * Z + z) for y in range(Y) for z in range(Z)]
    return lax.ppermute(a, "seq", perm)


def local(
    queries,
    keys,
    values,
    residual,
    out_weight,
    gate,
    mod_scale,
    mod_shift,
    frame_counts,
    patch_counts,
):
    s = lax.axis_index("seq")
    m = lax.axis_index("mp")
    x, core, y = m // CORES, m % CORES, s // Z

    barrier = lax.optimization_barrier
    own_weight = lax.ppermute(out_weight.T, ("seq", "mp"), weight_perm())
    packed = pack_kv(keys, values)
    packed, queries = barrier((packed, queries))
    right3, right1, left3, left1 = packed
    right3 = lax.ppermute(right3, "seq", ring_perm(1))
    left3 = lax.ppermute(left3, "seq", ring_perm(-1))
    right1 = lax.ppermute(right1, "seq", ring_perm(1))
    left1 = lax.ppermute(left1, "seq", ring_perm(-1))

    first = s * FR
    own_clips = clip_index(frame_counts, first + jnp.arange(FR, dtype=jnp.int32))
    clip_ids = jnp.arange(frame_counts.shape[0], dtype=jnp.int32)
    hot = own_clips[:, None] == clip_ids[None, :]
    own_grid = jnp.sum(jnp.where(hot, patch_counts[None, :], 0), axis=1)
    info = jnp.concatenate([own_clips, own_grid, jnp.stack([x, y, core]).astype(jnp.int32)])
    rel = [0, 1, 2, 3, -3, -2, -1, -4, 4, 5, 6, 7, -7, -6, -5, 8, 9, 10]
    rel = [r for r in rel for _ in range(GROUP)]
    key_ids = first + jnp.array(rel, dtype=jnp.int32)
    inside = (key_ids >= 0) & (key_ids < FR * Y * Z)
    key_clips = jnp.where(inside, clip_index(frame_counts, key_ids), -1)[None, :]

    even = even_attention(info, queries, keys, values)
    right3, left3, right1, left1, even, own_weight = barrier(
        (right3, left3, right1, left1, even, own_weight)
    )
    right6 = lax.ppermute(right3, "seq", ring_perm(1))
    left6 = lax.ppermute(left3, "seq", ring_perm(-1))
    weights = gather_weight(own_weight)
    even = spread(even)
    others = (right3, right1, left3, left1, right6, left6)
    odd = odd_attention(info, key_clips, queries, keys, values, others)
    odd, even = barrier((odd, even))
    odd = spread(odd)
    other_even = mp_move(jnp.concatenate(even, axis=0), 0, 1)
    other_odd = [mp_move(a, 0, 1) for a in odd]
    own_parts = [a for pair in zip(even, odd) for a in pair]
    operands = [*own_parts, other_even, *other_odd, weights]

    (far,) = project(info, operands, (2,), jnp.bfloat16)
    far, info = barrier((far, info))
    far = seq_move(far, 2)
    up, down = project(info, operands, (1, -1), jnp.bfloat16)
    up, down, info = barrier((up, down, info))
    up, down = seq_move(up, 1), seq_move(down, -1)
    (own,) = project(info, operands, (0,), jnp.float32)

    updated, squares = update(info, own, (far, up, down), residual, gate)
    squares = squares + mp_move(squares, 0, 1)
    normed = norm(info, updated, gather_x(squares), mod_scale, mod_shift)
    return updated, normed


def solution(mesh):
    in_specs = (
        P("seq", "mp"),
        P("seq", "mp"),
        P("seq", "mp"),
        P("seq", "mp"),
        P("mp", "seq"),
        P(None, "mp"),
        P(None, "mp"),
        P(None, "mp"),
        P(),
        P(),
    )
    out_specs = (P("seq", "mp"), P("seq", "mp"))
    return jax.shard_map(local, mesh=mesh, in_specs=in_specs, out_specs=out_specs, check_vma=False)
```

```python
import functools
import math

import jax
import jax.numpy as jnp
from jax import lax
from jax.experimental import pallas as pl
from jax.experimental.pallas import tpu as pltpu
from jax.sharding import PartitionSpec as P

D = 6144
HD = 128
S = 128
FR = 4
X, Y, Z, CORES = 4, 4, 8, 2
ROWS = FR * S
COLS = D // (X * CORES)
HALF = COLS // 2
WB = D // (Y * Z)
GROUP = 16
eps = 1e-06
negative = -1e30
NT = (((1,), (1,)), ((), ()))
HBM = pl.BlockSpec(memory_space=pltpu.HBM)
ROOM = pltpu.CompilerParams(vmem_limit_bytes=56 * 1024 * 1024)
TIGHT = pltpu.CompilerParams(vmem_limit_bytes=20 * 1024 * 1024)


def ring_perm(d):
    n = Y * Z
    return [(i, (i + d) % n) for i in range(n)]


def mp_perm(dx, dc):
    return [
        (x * CORES + c, (x + dx) % X * CORES + (c + dc) % CORES)
        for x in range(X)
        for c in range(CORES)
    ]


def device(x, y, z, c):
    return (y * Z + z) * X * CORES + x * CORES + c


PLACES = [(x, y, z, c) for x in range(X) for y in range(Y) for z in range(Z) for c in range(CORES)]


def weight_perm():
    half = Z // 2
    return [
        (device(x, y, z, c), device(y, x, z % half * CORES + c, z // half)) for x, y, z, c in PLACES
    ]


def spread_perm(shift):
    return [(device(x, y, z, c), device((y + shift) % X, x, z, c)) for x, y, z, c in PLACES]


def mp_move(a, dx, dc=0):
    return lax.ppermute(a, "mp", mp_perm(dx, dc))


def clip_index(frame_counts, frame_ids):
    ends = jnp.cumsum(frame_counts)
    return jnp.sum((ends[None, :] <= frame_ids[:, None]).astype(jnp.int32), axis=1)


def cost(flops, nbytes):
    return pl.CostEstimate(flops=flops, bytes_accessed=nbytes, transcendentals=0)


def pack_kv_kernel(k_ref, v_ref, r3_ref, r1_ref, l3_ref, l1_ref):
    for which, ref in enumerate((k_ref, v_ref)):
        r3_ref[which] = ref[1:]
        r1_ref[which] = ref[:1]
        l3_ref[which] = ref[: FR - 1]
        l1_ref[which] = ref[FR - 1 :]


def pack_kv(keys, values):
    sizes = (FR - 1, 1, FR - 1, 1)
    return pl.pallas_call(
        pack_kv_kernel,
        grid=(3,),
        in_specs=[pl.BlockSpec((FR, S, HD), lambda j: (0, 0, 2 * j + 1))] * 2,
        out_specs=[pl.BlockSpec((2, n, S, HD), lambda j: (0, 0, 0, j)) for n in sizes],
        out_shape=[jax.ShapeDtypeStruct((2, n, S, HALF), jnp.bfloat16) for n in sizes],
        compiler_params=ROOM,
        cost_estimate=cost(0, 6 * ROWS * HALF * 2),
        name="pack_kv",
    )(keys.reshape(FR, S, COLS), values.reshape(FR, S, COLS))


def softmax_weights(scores):
    highest = jnp.max(scores, axis=-1, keepdims=True)
    raised = jnp.exp(scores - highest)
    inverse = 1.0 / jnp.sum(raised, axis=-1, keepdims=True)
    return (raised * inverse).astype(jnp.bfloat16)


EVEN_FRAMES = 2


def even_kernel(info_ref, q_ref, k_ref, v_ref, o_ref):
    base = pl.program_id(0) * EVEN_FRAMES
    lane = lax.broadcasted_iota(jnp.int32, (S, S), 1)
    row = lax.broadcasted_iota(jnp.int32, (S, HD), 0)
    pieces = [(f, h) for f in range(EVEN_FRAMES) for h in range(3)]

    def take(ref, f, h):
        return ref[f * S : (f + 1) * S, 2 * h * HD : (2 * h + 1) * HD]

    scores = []
    for f, h in pieces:
        raw = lax.dot_general(
            take(q_ref, f, h), take(k_ref, f, h), NT, preferred_element_type=jnp.float32
        ) * (1.0 / math.sqrt(HD))
        scores.append(jnp.where(lane < info_ref[FR + base + f], raw, negative))
    weights = softmax_weights(jnp.concatenate(scores, axis=0))
    for i, (f, h) in enumerate(pieces):
        out = jnp.dot(
            weights[i * S : (i + 1) * S], take(v_ref, f, h), preferred_element_type=jnp.float32
        )
        out = jnp.where(row < info_ref[FR + base + f], out, 0.0).astype(jnp.bfloat16)
        o_ref[f * S : (f + 1) * S, h * HD : (h + 1) * HD] = out


def even_attention(info, queries, keys, values):
    block = pl.BlockSpec((EVEN_FRAMES * S, COLS), lambda f, g: (f, 0))
    return pl.pallas_call(
        even_kernel,
        grid_spec=pltpu.PrefetchScalarGridSpec(
            num_scalar_prefetch=1,
            grid=(FR // EVEN_FRAMES,),
            in_specs=[block] * 3,
            out_specs=pl.BlockSpec((EVEN_FRAMES * S, HALF), lambda f, g: (f, 0)),
        ),
        out_shape=jax.ShapeDtypeStruct((ROWS, HALF), jnp.bfloat16),
        compiler_params=ROOM,
        cost_estimate=cost(FR * 3 * 4 * S * S * HD, 4 * ROWS * COLS * 2),
        name="even_attention",
    )(info, queries, keys, values)


WINDOW = 18
BATCH = 2


def odd_kernel(info_ref, clip_ref, q_ref, k_ref, v_ref, *refs):
    far_refs, o_ref = refs[:-1], refs[-1]
    keys_wide = WINDOW * GROUP
    query_cell = lax.broadcasted_iota(jnp.int32, (GROUP, keys_wide), 0)
    key_cell = lax.rem(lax.broadcasted_iota(jnp.int32, (GROUP, keys_wide), 1), GROUP)
    same_cell = query_cell == key_cell
    allowed = [same_cell & (clip_ref[...] == info_ref[f]) for f in range(FR)]
    cell = lax.broadcasted_iota(jnp.int32, (GROUP, HD), 0)
    pieces = [(b, h) for b in range(BATCH) for h in range(3)]

    def window(own_ref, which, b, h):
        rows = slice(b * GROUP, (b + 1) * GROUP)
        wide = slice((2 * h + 1) * HD, (2 * h + 2) * HD)
        at = slice(h * HD, (h + 1) * HD)
        parts = [own_ref[:, rows, wide]]
        parts += [r[which, :, rows, at] for r in far_refs]
        return jnp.concatenate([p.reshape(-1, HD) for p in parts], axis=0)

    scores = []
    for b, h in pieces:
        q = q_ref[:, b * GROUP : (b + 1) * GROUP, (2 * h + 1) * HD : (2 * h + 2) * HD]
        raw = lax.dot_general(
            q.reshape(FR * GROUP, HD), window(k_ref, 0, b, h), NT,
            preferred_element_type=jnp.float32,
        ) * (1.0 / math.sqrt(HD))
        for f in range(FR):
            scores.append(jnp.where(allowed[f], raw[f * GROUP : (f + 1) * GROUP], negative))
    weights = softmax_weights(jnp.concatenate(scores, axis=0))
    n = FR * GROUP
    for i, (b, h) in enumerate(pieces):
        out = jnp.dot(
            weights[i * n : (i + 1) * n], window(v_ref, 1, b, h),
            preferred_element_type=jnp.float32,
        )
        first = (pl.program_id(0) * BATCH + b) * GROUP
        for f in range(FR):
            part = out[f * GROUP : (f + 1) * GROUP]
            part = jnp.where(first + cell < info_ref[FR + f], part, 0.0)
            o_ref[f, b * GROUP : (b + 1) * GROUP, h * HD : (h + 1) * HD] = part.astype(
                jnp.bfloat16
            )


def odd_attention(info, key_clips, queries, keys, values, others):
    def frames(a):
        return a.reshape(FR, S, COLS)

    step = GROUP * BATCH
    own = pl.BlockSpec((FR, step, COLS), lambda i, g: (0, i, 0))

    def other(n):
        return pl.BlockSpec((2, n, step, HALF), lambda i, g: (0, 0, i, 0))

    out = pl.pallas_call(
        odd_kernel,
        grid_spec=pltpu.PrefetchScalarGridSpec(
            num_scalar_prefetch=1,
            grid=(S // step,),
            in_specs=[
                pl.BlockSpec((1, WINDOW * GROUP), lambda i, g: (0, 0)),
                own, own, own, *[other(a.shape[1]) for a in others],
            ],
            out_specs=pl.BlockSpec((FR, step, HALF), lambda i, g: (0, i, 0)),
        ),
        out_shape=jax.ShapeDtypeStruct((FR, S, HALF), jnp.bfloat16),
        compiler_params=ROOM,
        cost_estimate=cost(ROWS * 3 * 4 * WINDOW * GROUP * HD, 10 * ROWS * COLS * 2),
        name="odd_attention",
    )(info, key_clips, frames(queries), frames(keys), frames(values), *others)
    return out.reshape(ROWS, HALF)


def project_kernel(shifts, info_ref, *refs):
    own_refs, other_even, other_odd = refs[: 2 * X], refs[2 * X : 3 * X], refs[3 * X : 4 * X]
    w_ref = refs[4 * X]
    n = len(shifts)
    o_refs, (a_buf, w_buf, a_sem, w_sem) = refs[4 * X + 1 : 4 * X + 1 + n], refs[4 * X + 1 + n :]
    x, y, core = info_ref[2 * FR], info_ref[2 * FR + 1], info_ref[2 * FR + 2]
    half = Z // 2
    w_copies = [
        pltpu.make_async_copy(
            w_ref.at[CORES * i + c], w_buf.at[i, :, c * COLS : (c + 1) * COLS], w_sem.at[i]
        )
        for i in range(half)
        for c in range(CORES)
    ]
    for copy in w_copies:
        copy.start()
    for i, d in enumerate(shifts):
        slot = lax.rem(x - y - d + 2 * X, X)
        for r in range(X):
            sources = [own_refs[2 * r], own_refs[2 * r + 1]]
            sources += [other_even[r], other_odd[r]]

            @pl.when(slot == r)
            def _(sources=sources, i=i):
                for k, source in enumerate(sources):
                    side = core if k < 2 else 1 - core
                    for h in range(3):
                        at = pl.multiple_of(side * COLS + (2 * h + k % 2) * HD, HD)
                        pltpu.make_async_copy(
                            source.at[:, h * HD : (h + 1) * HD],
                            a_buf.at[i, :, pl.ds(at, HD)],
                            a_sem.at[i],
                        ).start()
    for copy in w_copies:
        copy.wait()
    for i in range(n):
        pltpu.make_async_copy(a_buf.at[i], a_buf.at[i], a_sem.at[i]).wait()
        total = lax.dot_general(
            a_buf[i], w_buf[...].reshape(COLS, 2 * COLS), NT, preferred_element_type=jnp.float32
        )
        o_refs[i][...] = total.astype(o_refs[i].dtype)


def project(info, operands, shifts, out_type):
    n = len(shifts)
    return pl.pallas_call(
        functools.partial(project_kernel, shifts),
        grid_spec=pltpu.PrefetchScalarGridSpec(
            num_scalar_prefetch=1,
            grid=(1,),
            in_specs=[HBM] * len(operands),
            out_specs=[pl.BlockSpec((ROWS, COLS), lambda i, p: (0, 0))] * n,
            scratch_shapes=[
                pltpu.VMEM((n, ROWS, 2 * COLS), jnp.bfloat16),
                pltpu.VMEM((Z // 2, WB, 2 * COLS), jnp.bfloat16),
                pltpu.SemaphoreType.DMA((n,)),
                pltpu.SemaphoreType.DMA((Z // 2,)),
            ],
        ),
        out_shape=[jax.ShapeDtypeStruct((ROWS, COLS), out_type)] * n,
        compiler_params=ROOM,
        cost_estimate=cost(4 * n * ROWS * COLS * COLS, 4 * 1024 * 1024),
        name="project",
    )(info, *operands)


TAIL_FRAMES = 2


def table_row(table_ref, clip):
    lane = lax.broadcasted_iota(jnp.int32, (8, table_ref.shape[0]), 1)
    hot = jnp.where(lane == clip, 1.0, 0.0).astype(jnp.bfloat16)
    return jnp.dot(hot, table_ref[...], preferred_element_type=jnp.float32)[:1]


def update_kernel(
    info_ref, own_ref, p0_ref, p1_ref, p2_ref, residual_ref, gate_ref, u_ref, sq_ref
):
    for f in range(TAIL_FRAMES):
        rows = slice(f * S, (f + 1) * S)
        gate = table_row(gate_ref, info_ref[pl.program_id(0) * TAIL_FRAMES + f])
        folded = None
        for j in range(COLS // HD):
            at = slice(j * HD, (j + 1) * HD)
            total = own_ref[rows, at]
            for part_ref in (p0_ref, p1_ref, p2_ref):
                total = total + part_ref[rows, at].astype(jnp.float32)
            combined = residual_ref[rows, at].astype(jnp.float32) + gate[:, at] * total
            updated = combined.astype(jnp.bfloat16)
            u_ref[rows, at] = updated
            wide = updated.astype(jnp.float32)
            folded = wide * wide if folded is None else folded + wide * wide
        sq_ref[f] = jnp.sum(folded.T, axis=0, keepdims=True)


def update(info, own, parts, residual, gate):
    block = pl.BlockSpec((TAIL_FRAMES * S, COLS), lambda f, g: (f, 0))
    return pl.pallas_call(
        update_kernel,
        grid_spec=pltpu.PrefetchScalarGridSpec(
            num_scalar_prefetch=1,
            grid=(FR // TAIL_FRAMES,),
            in_specs=[block] * 5 + [pl.BlockSpec(gate.shape, lambda f, g: (0, 0))],
            out_specs=[block, pl.BlockSpec((TAIL_FRAMES, 1, S), lambda f, g: (f, 0, 0))],
        ),
        out_shape=[
            jax.ShapeDtypeStruct((ROWS, COLS), jnp.bfloat16),
            jax.ShapeDtypeStruct((FR, 1, S), jnp.float32),
        ],
        compiler_params=TIGHT,
        cost_estimate=cost(0, ROWS * COLS * 14),
        name="update",
    )(info, own, *parts, residual, gate)


def norm_kernel(info_ref, u_ref, s0_ref, s1_ref, s2_ref, s3_ref, scale_ref, shift_ref, o_ref):
    for f in range(TAIL_FRAMES):
        rows = slice(f * S, (f + 1) * S)
        clip = info_ref[pl.program_id(0) * TAIL_FRAMES + f]
        scale, shift = table_row(scale_ref, clip), table_row(shift_ref, clip)
        total = s0_ref[f] + s1_ref[f] + s2_ref[f] + s3_ref[f]
        inverse = lax.rsqrt(total * (1.0 / D) + eps)
        inverse = jnp.broadcast_to(inverse, (S, S)).T
        for j in range(COLS // HD):
            at = slice(j * HD, (j + 1) * HD)
            wide = u_ref[rows, at].astype(jnp.float32)
            normed = wide * inverse * (1.0 + scale[:, at]) + shift[:, at]
            o_ref[rows, at] = normed.astype(jnp.bfloat16)


def norm(info, updated, sums, scale, shift):
    block = pl.BlockSpec((TAIL_FRAMES * S, COLS), lambda f, g: (f, 0))
    table = pl.BlockSpec(scale.shape, lambda f, g: (0, 0))
    lane = pl.BlockSpec((TAIL_FRAMES, 1, S), lambda f, g: (f, 0, 0))
    return pl.pallas_call(
        norm_kernel,
        grid_spec=pltpu.PrefetchScalarGridSpec(
            num_scalar_prefetch=1,
            grid=(FR // TAIL_FRAMES,),
            in_specs=[block, lane, lane, lane, lane, table, table],
            out_specs=block,
        ),
        out_shape=jax.ShapeDtypeStruct((ROWS, COLS), jnp.bfloat16),
        compiler_params=ROOM,
        cost_estimate=cost(0, ROWS * COLS * 4),
        name="norm",
    )(info, updated, *sums, scale, shift)


def gather_weight(own):
    groups = [[y * Z + z for z in range(Z)] for y in range(Y)]
    return lax.all_gather(own, "seq", axis=0, tiled=False, axis_index_groups=groups)


def spread(a, shift):
    return lax.ppermute(a, ("seq", "mp"), spread_perm(shift))


def gather_x(a):
    return [a, mp_move(a, -1), mp_move(a, 2), mp_move(a, 1)]


def seq_move(a, dy):
    perm = [(y * Z + z, (y + dy) % Y * Z + z) for y in range(Y) for z in range(Z)]
    return lax.ppermute(a, "seq", perm)


def local(
    queries,
    keys,
    values,
    residual,
    out_weight,
    gate,
    mod_scale,
    mod_shift,
    frame_counts,
    patch_counts,
):
    s = lax.axis_index("seq")
    m = lax.axis_index("mp")
    x, core, y = m // CORES, m % CORES, s // Z

    barrier = lax.optimization_barrier
    own_weight = lax.ppermute(out_weight.T, ("seq", "mp"), weight_perm())
    packed = pack_kv(keys, values)
    packed, queries = barrier((packed, queries))
    right3, right1, left3, left1 = packed
    right3 = lax.ppermute(right3, "seq", ring_perm(1))
    left3 = lax.ppermute(left3, "seq", ring_perm(-1))
    right1 = lax.ppermute(right1, "seq", ring_perm(1))
    left1 = lax.ppermute(left1, "seq", ring_perm(-1))

    first = s * FR
    own_clips = clip_index(frame_counts, first + jnp.arange(FR, dtype=jnp.int32))
    clip_ids = jnp.arange(frame_counts.shape[0], dtype=jnp.int32)
    hot = own_clips[:, None] == clip_ids[None, :]
    own_grid = jnp.sum(jnp.where(hot, patch_counts[None, :], 0), axis=1)
    info = jnp.concatenate([own_clips, own_grid, jnp.stack([x, y, core]).astype(jnp.int32)])
    rel = [0, 1, 2, 3, -3, -2, -1, -4, 4, 5, 6, 7, -7, -6, -5, 8, 9, 10]
    rel = [r for r in rel for _ in range(GROUP)]
    key_ids = first + jnp.array(rel, dtype=jnp.int32)
    inside = (key_ids >= 0) & (key_ids < FR * Y * Z)
    key_clips = jnp.where(inside, clip_index(frame_counts, key_ids), -1)[None, :]

    even = even_attention(info, queries, keys, values)
    right3, left3, right1, left1, even, own_weight = barrier(
        (right3, left3, right1, left1, even, own_weight)
    )
    right6 = lax.ppermute(right3, "seq", ring_perm(1))
    left6 = lax.ppermute(left3, "seq", ring_perm(-1))
    weights = gather_weight(own_weight)
    early = [spread(even, r) for r in range(1, X)]
    others = (right3, right1, left3, left1, right6, left6)
    odd = odd_attention(info, key_clips, queries, keys, values, others)
    odd, even = barrier((odd, even))
    odd = [spread(odd, r) for r in range(X)]
    early, _ = barrier((early, odd[X - 1]))
    even = [spread(even, 0)] + early
    other_even = [mp_move(a, 0, 1) for a in even]
    other_odd = [mp_move(a, 0, 1) for a in odd]
    own_parts = [a for pair in zip(even, odd) for a in pair]
    operands = [*own_parts, *other_even, *other_odd, weights]

    (far,) = project(info, operands, (2,), jnp.bfloat16)
    far, info = barrier((far, info))
    far = seq_move(far, 2)
    up, down = project(info, operands, (1, -1), jnp.bfloat16)
    up, down, info = barrier((up, down, info))
    up, down = seq_move(up, 1), seq_move(down, -1)
    (own,) = project(info, operands, (0,), jnp.float32)

    updated, squares = update(info, own, (far, up, down), residual, gate)
    squares = squares + mp_move(squares, 0, 1)
    normed = norm(info, updated, gather_x(squares), mod_scale, mod_shift)
    return updated, normed


def solution(mesh):
    in_specs = (
        P("seq", "mp"),
        P("seq", "mp"),
        P("seq", "mp"),
        P("seq", "mp"),
        P("mp", "seq"),
        P(None, "mp"),
        P(None, "mp"),
        P(None, "mp"),
        P(),
        P(),
    )
    out_specs = (P("seq", "mp"), P("seq", "mp"))
    return jax.shard_map(local, mesh=mesh, in_specs=in_specs, out_specs=out_specs, check_vma=False)
```

```python
import functools
import math

import jax
import jax.numpy as jnp
from jax import lax
from jax.experimental import pallas as pl
from jax.experimental.pallas import tpu as pltpu
from jax.sharding import PartitionSpec as P

D = 6144
HD = 128
S = 128
FR = 4
X, Y, Z, CORES = 4, 4, 8, 2
ROWS = FR * S
COLS = D // (X * CORES)
HALF = COLS // 2
WB = D // (Y * Z)
GROUP = 16
eps = 1e-06
negative = -1e30
NT = (((1,), (1,)), ((), ()))
HBM = pl.BlockSpec(memory_space=pltpu.HBM)
ROOM = pltpu.CompilerParams(vmem_limit_bytes=56 * 1024 * 1024)
MIDDLE = pltpu.CompilerParams(vmem_limit_bytes=52 * 1024 * 1024)
TIGHT = pltpu.CompilerParams(vmem_limit_bytes=20 * 1024 * 1024)


def ring_perm(d):
    n = Y * Z
    return [(i, (i + d) % n) for i in range(n)]


def mp_perm(dx, dc):
    return [
        (x * CORES + c, (x + dx) % X * CORES + (c + dc) % CORES)
        for x in range(X)
        for c in range(CORES)
    ]


def device(x, y, z, c):
    return (y * Z + z) * X * CORES + x * CORES + c


PLACES = [(x, y, z, c) for x in range(X) for y in range(Y) for z in range(Z) for c in range(CORES)]


def weight_perm():
    half = Z // 2
    return [
        (device(x, y, z, c), device(y, x, z % half * CORES + c, z // half)) for x, y, z, c in PLACES
    ]


def spread_perm(shift):
    return [(device(x, y, z, c), device((y + shift) % X, x, z, c)) for x, y, z, c in PLACES]


def mp_move(a, dx, dc=0):
    return lax.ppermute(a, "mp", mp_perm(dx, dc))


def clip_index(frame_counts, frame_ids):
    ends = jnp.cumsum(frame_counts)
    return jnp.sum((ends[None, :] <= frame_ids[:, None]).astype(jnp.int32), axis=1)


def cost(flops, nbytes):
    return pl.CostEstimate(flops=flops, bytes_accessed=nbytes, transcendentals=0)


def pack_kv_kernel(*refs):
    r3_ref, r1_ref, l3_ref, l1_ref = refs[6:]
    for i, ref in enumerate(refs[:6]):
        which, at = i // 3, slice(i % 3 * HD, (i % 3 + 1) * HD)
        r3_ref[which, :, :, at] = ref[1:]
        r1_ref[which, :, :, at] = ref[:1]
        l3_ref[which, :, :, at] = ref[: FR - 1]
        l1_ref[which, :, :, at] = ref[FR - 1 :]


def pack_kv(keys, values):
    sizes = (FR - 1, 1, FR - 1, 1)
    heads = [pl.BlockSpec((FR, S, HD), lambda i, j=j: (0, 0, 2 * j + 1)) for j in range(3)]
    keys, values = keys.reshape(FR, S, COLS), values.reshape(FR, S, COLS)
    return pl.pallas_call(
        pack_kv_kernel,
        grid=(1,),
        in_specs=heads * 2,
        out_specs=[pl.BlockSpec((2, n, S, HALF), lambda i: (0, 0, 0, 0)) for n in sizes],
        out_shape=[jax.ShapeDtypeStruct((2, n, S, HALF), jnp.bfloat16) for n in sizes],
        compiler_params=ROOM,
        cost_estimate=cost(0, 6 * ROWS * HALF * 2),
        name="pack_kv",
    )(keys, keys, keys, values, values, values)


def softmax_weights(scores):
    highest = jnp.max(scores, axis=-1, keepdims=True)
    raised = jnp.exp(scores - highest)
    inverse = 1.0 / jnp.sum(raised, axis=-1, keepdims=True)
    return (raised * inverse).astype(jnp.bfloat16)


EVEN_FRAMES = 2


def even_kernel(info_ref, q_ref, k_ref, v_ref, o_ref):
    base = pl.program_id(0) * EVEN_FRAMES
    lane = lax.broadcasted_iota(jnp.int32, (S, S), 1)
    row = lax.broadcasted_iota(jnp.int32, (S, HD), 0)
    pieces = [(f, h) for f in range(EVEN_FRAMES) for h in range(3)]

    def take(ref, f, h):
        return ref[f * S : (f + 1) * S, 2 * h * HD : (2 * h + 1) * HD]

    scores = []
    for f, h in pieces:
        raw = lax.dot_general(
            take(q_ref, f, h), take(k_ref, f, h), NT, preferred_element_type=jnp.float32
        ) * (1.0 / math.sqrt(HD))
        scores.append(jnp.where(lane < info_ref[FR + base + f], raw, negative))
    weights = softmax_weights(jnp.concatenate(scores, axis=0))
    for i, (f, h) in enumerate(pieces):
        out = jnp.dot(
            weights[i * S : (i + 1) * S], take(v_ref, f, h), preferred_element_type=jnp.float32
        )
        out = jnp.where(row < info_ref[FR + base + f], out, 0.0).astype(jnp.bfloat16)
        o_ref[f * S : (f + 1) * S, h * HD : (h + 1) * HD] = out


def even_attention(info, queries, keys, values):
    block = pl.BlockSpec((EVEN_FRAMES * S, COLS), lambda f, g: (f, 0))
    return pl.pallas_call(
        even_kernel,
        grid_spec=pltpu.PrefetchScalarGridSpec(
            num_scalar_prefetch=1,
            grid=(FR // EVEN_FRAMES,),
            in_specs=[block] * 3,
            out_specs=pl.BlockSpec((EVEN_FRAMES * S, HALF), lambda f, g: (f, 0)),
        ),
        out_shape=jax.ShapeDtypeStruct((ROWS, HALF), jnp.bfloat16),
        compiler_params=ROOM,
        cost_estimate=cost(FR * 3 * 4 * S * S * HD, 4 * ROWS * COLS * 2),
        name="even_attention",
    )(info, queries, keys, values)


WINDOW = 18
BATCH = 2


def odd_kernel(info_ref, clip_ref, q_ref, k_ref, v_ref, *refs):
    far_refs, o_ref = refs[:-1], refs[-1]
    keys_wide = WINDOW * GROUP
    query_cell = lax.broadcasted_iota(jnp.int32, (GROUP, keys_wide), 0)
    key_cell = lax.rem(lax.broadcasted_iota(jnp.int32, (GROUP, keys_wide), 1), GROUP)
    same_cell = query_cell == key_cell
    allowed = [same_cell & (clip_ref[...] == info_ref[f]) for f in range(FR)]
    cell = lax.broadcasted_iota(jnp.int32, (GROUP, HD), 0)
    pieces = [(b, h) for b in range(BATCH) for h in range(3)]

    def window(own_ref, which, b, h):
        rows = slice(b * GROUP, (b + 1) * GROUP)
        wide = slice((2 * h + 1) * HD, (2 * h + 2) * HD)
        at = slice(h * HD, (h + 1) * HD)
        parts = [own_ref[:, rows, wide]]
        parts += [r[which, :, rows, at] for r in far_refs]
        return jnp.concatenate([p.reshape(-1, HD) for p in parts], axis=0)

    scores = []
    for b, h in pieces:
        q = q_ref[:, b * GROUP : (b + 1) * GROUP, (2 * h + 1) * HD : (2 * h + 2) * HD]
        raw = lax.dot_general(
            q.reshape(FR * GROUP, HD), window(k_ref, 0, b, h), NT,
            preferred_element_type=jnp.float32,
        ) * (1.0 / math.sqrt(HD))
        for f in range(FR):
            scores.append(jnp.where(allowed[f], raw[f * GROUP : (f + 1) * GROUP], negative))
    weights = softmax_weights(jnp.concatenate(scores, axis=0))
    n = FR * GROUP
    for i, (b, h) in enumerate(pieces):
        out = jnp.dot(
            weights[i * n : (i + 1) * n], window(v_ref, 1, b, h),
            preferred_element_type=jnp.float32,
        )
        first = (pl.program_id(0) * BATCH + b) * GROUP
        for f in range(FR):
            part = out[f * GROUP : (f + 1) * GROUP]
            part = jnp.where(first + cell < info_ref[FR + f], part, 0.0)
            o_ref[f, b * GROUP : (b + 1) * GROUP, h * HD : (h + 1) * HD] = part.astype(
                jnp.bfloat16
            )


def odd_attention(info, key_clips, queries, keys, values, others):
    def frames(a):
        return a.reshape(FR, S, COLS)

    step = GROUP * BATCH
    own = pl.BlockSpec((FR, step, COLS), lambda i, g: (0, i, 0))

    def other(n):
        return pl.BlockSpec((2, n, step, HALF), lambda i, g: (0, 0, i, 0))

    out = pl.pallas_call(
        odd_kernel,
        grid_spec=pltpu.PrefetchScalarGridSpec(
            num_scalar_prefetch=1,
            grid=(S // step,),
            in_specs=[
                pl.BlockSpec((1, WINDOW * GROUP), lambda i, g: (0, 0)),
                own, own, own, *[other(a.shape[1]) for a in others],
            ],
            out_specs=pl.BlockSpec((FR, step, HALF), lambda i, g: (0, i, 0)),
        ),
        out_shape=jax.ShapeDtypeStruct((FR, S, HALF), jnp.bfloat16),
        compiler_params=TIGHT,
        cost_estimate=cost(ROWS * 3 * 4 * WINDOW * GROUP * HD, 10 * ROWS * COLS * 2),
        name="odd_attention",
    )(info, key_clips, frames(queries), frames(keys), frames(values), *others)
    return out.reshape(ROWS, HALF)


def project_kernel(shifts, info_ref, *refs):
    own_refs, other_even, other_odd = refs[: 2 * X], refs[2 * X : 3 * X], refs[3 * X : 4 * X]
    w_ref = refs[4 * X]
    n = len(shifts)
    o_refs, (a_buf, w_buf, a_sem, w_sem) = refs[4 * X + 1 : 4 * X + 1 + n], refs[4 * X + 1 + n :]
    x, y, core = info_ref[2 * FR], info_ref[2 * FR + 1], info_ref[2 * FR + 2]
    half = Z // 2
    w_copies = [
        pltpu.make_async_copy(
            w_ref.at[CORES * i + c], w_buf.at[i, :, c * COLS : (c + 1) * COLS], w_sem.at[i]
        )
        for i in range(half)
        for c in range(CORES)
    ]
    for copy in w_copies:
        copy.start()
    for i, d in enumerate(shifts):
        slot = lax.rem(x - y - d + 2 * X, X)
        for r in range(X):
            sources = [own_refs[2 * r], own_refs[2 * r + 1]]
            sources += [other_even[r], other_odd[r]]

            @pl.when(slot == r)
            def _(sources=sources, i=i):
                for k, source in enumerate(sources):
                    side = core if k < 2 else 1 - core
                    for h in range(3):
                        at = pl.multiple_of(side * COLS + (2 * h + k % 2) * HD, HD)
                        pltpu.make_async_copy(
                            source.at[:, h * HD : (h + 1) * HD],
                            a_buf.at[i, :, pl.ds(at, HD)],
                            a_sem.at[i],
                        ).start()
    for copy in w_copies:
        copy.wait()
    for i in range(n):
        pltpu.make_async_copy(a_buf.at[i], a_buf.at[i], a_sem.at[i]).wait()
        total = lax.dot_general(
            a_buf[i], w_buf[...].reshape(COLS, 2 * COLS), NT, preferred_element_type=jnp.float32
        )
        o_refs[i][...] = total.astype(o_refs[i].dtype)


def project(info, operands, shifts, out_type):
    n = len(shifts)
    return pl.pallas_call(
        functools.partial(project_kernel, shifts),
        grid_spec=pltpu.PrefetchScalarGridSpec(
            num_scalar_prefetch=1,
            grid=(1,),
            in_specs=[HBM] * len(operands),
            out_specs=[pl.BlockSpec((ROWS, COLS), lambda i, p: (0, 0))] * n,
            scratch_shapes=[
                pltpu.VMEM((n, ROWS, 2 * COLS), jnp.bfloat16),
                pltpu.VMEM((Z // 2, WB, 2 * COLS), jnp.bfloat16),
                pltpu.SemaphoreType.DMA((n,)),
                pltpu.SemaphoreType.DMA((Z // 2,)),
            ],
        ),
        out_shape=[jax.ShapeDtypeStruct((ROWS, COLS), out_type)] * n,
        compiler_params=MIDDLE,
        cost_estimate=cost(4 * n * ROWS * COLS * COLS, 4 * 1024 * 1024),
        name="project",
    )(info, *operands)


TAIL_FRAMES = 2


def table_row(table_ref, clip):
    lane = lax.broadcasted_iota(jnp.int32, (8, table_ref.shape[0]), 1)
    hot = jnp.where(lane == clip, 1.0, 0.0).astype(jnp.bfloat16)
    return jnp.dot(hot, table_ref[...], preferred_element_type=jnp.float32)[:1]


def update_kernel(
    info_ref, own_ref, p0_ref, p1_ref, p2_ref, residual_ref, gate_ref, u_ref, sq_ref
):
    for f in range(TAIL_FRAMES):
        rows = slice(f * S, (f + 1) * S)
        gate = table_row(gate_ref, info_ref[pl.program_id(0) * TAIL_FRAMES + f])
        folded = None
        for j in range(COLS // HD):
            at = slice(j * HD, (j + 1) * HD)
            total = own_ref[rows, at]
            for part_ref in (p0_ref, p1_ref, p2_ref):
                total = total + part_ref[rows, at].astype(jnp.float32)
            combined = residual_ref[rows, at].astype(jnp.float32) + gate[:, at] * total
            updated = combined.astype(jnp.bfloat16)
            u_ref[rows, at] = updated
            wide = updated.astype(jnp.float32)
            folded = wide * wide if folded is None else folded + wide * wide
        sq_ref[f] = jnp.sum(folded.T, axis=0, keepdims=True)


def update(info, own, parts, residual, gate):
    block = pl.BlockSpec((TAIL_FRAMES * S, COLS), lambda f, g: (f, 0))
    return pl.pallas_call(
        update_kernel,
        grid_spec=pltpu.PrefetchScalarGridSpec(
            num_scalar_prefetch=1,
            grid=(FR // TAIL_FRAMES,),
            in_specs=[block] * 5 + [pl.BlockSpec(gate.shape, lambda f, g: (0, 0))],
            out_specs=[block, pl.BlockSpec((TAIL_FRAMES, 1, S), lambda f, g: (f, 0, 0))],
        ),
        out_shape=[
            jax.ShapeDtypeStruct((ROWS, COLS), jnp.bfloat16),
            jax.ShapeDtypeStruct((FR, 1, S), jnp.float32),
        ],
        compiler_params=TIGHT,
        cost_estimate=cost(0, ROWS * COLS * 14),
        name="update",
    )(info, own, *parts, residual, gate)


def norm_kernel(info_ref, u_ref, s0_ref, s1_ref, s2_ref, s3_ref, scale_ref, shift_ref, o_ref):
    for f in range(TAIL_FRAMES):
        rows = slice(f * S, (f + 1) * S)
        clip = info_ref[pl.program_id(0) * TAIL_FRAMES + f]
        scale, shift = table_row(scale_ref, clip), table_row(shift_ref, clip)
        total = s0_ref[f] + s1_ref[f] + s2_ref[f] + s3_ref[f]
        inverse = lax.rsqrt(total * (1.0 / D) + eps)
        inverse = jnp.broadcast_to(inverse, (S, S)).T
        for j in range(COLS // HD):
            at = slice(j * HD, (j + 1) * HD)
            wide = u_ref[rows, at].astype(jnp.float32)
            normed = wide * inverse * (1.0 + scale[:, at]) + shift[:, at]
            o_ref[rows, at] = normed.astype(jnp.bfloat16)


def norm(info, updated, sums, scale, shift):
    block = pl.BlockSpec((TAIL_FRAMES * S, COLS), lambda f, g: (f, 0))
    table = pl.BlockSpec(scale.shape, lambda f, g: (0, 0))
    lane = pl.BlockSpec((TAIL_FRAMES, 1, S), lambda f, g: (f, 0, 0))
    return pl.pallas_call(
        norm_kernel,
        grid_spec=pltpu.PrefetchScalarGridSpec(
            num_scalar_prefetch=1,
            grid=(FR // TAIL_FRAMES,),
            in_specs=[block, lane, lane, lane, lane, table, table],
            out_specs=block,
        ),
        out_shape=jax.ShapeDtypeStruct((ROWS, COLS), jnp.bfloat16),
        compiler_params=TIGHT,
        cost_estimate=cost(0, ROWS * COLS * 4),
        name="norm",
    )(info, updated, *sums, scale, shift)


def gather_weight(own):
    groups = [[y * Z + z for z in range(Z)] for y in range(Y)]
    return lax.all_gather(own, "seq", axis=0, tiled=False, axis_index_groups=groups)


def spread(a, shift):
    return lax.ppermute(a, ("seq", "mp"), spread_perm(shift))


def gather_x(a):
    return [a, mp_move(a, -1), mp_move(a, 2), mp_move(a, 1)]


def seq_move(a, dy):
    perm = [(y * Z + z, (y + dy) % Y * Z + z) for y in range(Y) for z in range(Z)]
    return lax.ppermute(a, "seq", perm)


def local(
    queries,
    keys,
    values,
    residual,
    out_weight,
    gate,
    mod_scale,
    mod_shift,
    frame_counts,
    patch_counts,
):
    s = lax.axis_index("seq")
    m = lax.axis_index("mp")
    x, core, y = m // CORES, m % CORES, s // Z

    barrier = lax.optimization_barrier
    own_weight = lax.ppermute(out_weight.T, ("seq", "mp"), weight_perm())
    packed = pack_kv(keys, values)
    packed, queries = barrier((packed, queries))
    right3, right1, left3, left1 = packed
    right3 = lax.ppermute(right3, "seq", ring_perm(1))
    left3 = lax.ppermute(left3, "seq", ring_perm(-1))
    right1 = lax.ppermute(right1, "seq", ring_perm(1))
    left1 = lax.ppermute(left1, "seq", ring_perm(-1))

    first = s * FR
    own_clips = clip_index(frame_counts, first + jnp.arange(FR, dtype=jnp.int32))
    clip_ids = jnp.arange(frame_counts.shape[0], dtype=jnp.int32)
    hot = own_clips[:, None] == clip_ids[None, :]
    own_grid = jnp.sum(jnp.where(hot, patch_counts[None, :], 0), axis=1)
    info = jnp.concatenate([own_clips, own_grid, jnp.stack([x, y, core]).astype(jnp.int32)])
    rel = [0, 1, 2, 3, -3, -2, -1, -4, 4, 5, 6, 7, -7, -6, -5, 8, 9, 10]
    rel = [r for r in rel for _ in range(GROUP)]
    key_ids = first + jnp.array(rel, dtype=jnp.int32)
    inside = (key_ids >= 0) & (key_ids < FR * Y * Z)
    key_clips = jnp.where(inside, clip_index(frame_counts, key_ids), -1)[None, :]

    even = even_attention(info, queries, keys, values)
    right3, left3, right1, left1, even, own_weight = barrier(
        (right3, left3, right1, left1, even, own_weight)
    )
    right6 = lax.ppermute(right3, "seq", ring_perm(1))
    left6 = lax.ppermute(left3, "seq", ring_perm(-1))
    weights = gather_weight(own_weight)
    early = [spread(even, r) for r in range(1, X)]
    others = (right3, right1, left3, left1, right6, left6)
    odd = odd_attention(info, key_clips, queries, keys, values, others)
    odd, even = barrier((odd, even))
    odd = [spread(odd, r) for r in range(X)]
    early, _ = barrier((early, odd[X - 1]))
    even = [spread(even, 0)] + early
    other_even = [mp_move(a, 0, 1) for a in even]
    other_odd = [mp_move(a, 0, 1) for a in odd]
    own_parts = [a for pair in zip(even, odd) for a in pair]
    operands = [*own_parts, *other_even, *other_odd, weights]

    (far,) = project(info, operands, (2,), jnp.bfloat16)
    far, info = barrier((far, info))
    far = seq_move(far, 2)
    up, down = project(info, operands, (1, -1), jnp.bfloat16)
    up, down, info = barrier((up, down, info))
    up, down = seq_move(up, 1), seq_move(down, -1)
    (own,) = project(info, operands, (0,), jnp.float32)

    updated, squares = update(info, own, (far, up, down), residual, gate)
    squares = squares + mp_move(squares, 0, 1)
    normed = norm(info, updated, gather_x(squares), mod_scale, mod_shift)
    return updated, normed


def solution(mesh):
    in_specs = (
        P("seq", "mp"),
        P("seq", "mp"),
        P("seq", "mp"),
        P("seq", "mp"),
        P("mp", "seq"),
        P(None, "mp"),
        P(None, "mp"),
        P(None, "mp"),
        P(),
        P(),
    )
    out_specs = (P("seq", "mp"), P("seq", "mp"))
    return jax.shard_map(local, mesh=mesh, in_specs=in_specs, out_specs=out_specs, check_vma=False)
```
